32 devices in a mesh: layer: 4 (over y, x), phi: 8 (over z, core).
Axes of the slice: x: 2, y: 2, z: 4, core: 2. Of those that a mesh axis runs over, the one named last changes fastest.
Arguments:
- hits: bfloat16 [4, 8, 8192, 128], P('layer', 'phi'), may hold values from -6 to 6
- attach_index: int32 [4, 8, 4, 8192], P('layer', 'phi'), may hold values from 0 to 1023, as said below
- attach_weight: bfloat16 [4, 8, 4, 8192], P('layer', 'phi'), may hold values from 0.049804688 to 1
- shard_counts: int32 [4, 8], P('layer', 'phi'), may hold values from 1024 to 8192, as said below
- edge_source: int32 [8, 8, 1024], P('phi'), may hold values from 0 to 2047
- cotangent: bfloat16 [8, 1024, 128], P('phi'), may hold values from -12 to 12
- w_message: bfloat16 [128, 128], replicated, may hold values from -0.5 to 0.5
- w_edge: bfloat16 [128, 128], replicated, may hold values from -0.5 to 0.5
- w_output: bfloat16 [128, 128], replicated, may hold values from -0.5 to 0.5
Outputs:
- d_hits: bfloat16 [4, 8, 8192, 128], P('layer', 'phi')
- grad_message: float32 [128, 128], replicated
- grad_edge: float32 [128, 128], replicated
- grad_output: float32 [128, 128], replicated
The draws below stay inside these ranges and needn't reach their ends.
Inputs may be any that keep to these rules, and one draw needn't show every extreme that they name: `attach_index`: A hit's four super-nodes are different. `shard_counts`: slots from the count on are padding; at least one shard is full. `edge_source`: row r of a sector's extended list is the previous sector's super-node 1024 - 512 + r for r < 512, its own super-node r - 512 below 1536, and else the next sector's super-node r - 1536.
All inputs are finite; a program needn't handle non-finite values.
Results may differ from the reference program's by a relative error of at most 0.015.
Values may be sent and summed in bfloat16 or wider, within the bound.
A program may use at most 64 MiB of HBM per device.

```python
import math
import jax
import jax.numpy as jnp
from jax import lax

WIDTH = 128
HIT_DEV = 8192
SN_COL = 1024
DEG = 8
RIM = 512
LAYERS = 4
SECTORS = 8


def draw_attach_index(key, part):
    first_key, second_key = jax.random.split(key)
    anchor = jax.random.randint(first_key, (LAYERS, SECTORS, 1, HIT_DEV), 0, SN_COL)
    stride = jax.random.randint(second_key, (LAYERS, SECTORS, 1, HIT_DEV), 1, SN_COL // 4 + 1)
    ranks = jnp.arange(4, dtype=jnp.int32).reshape(1, 1, 4, 1)
    return ((anchor + ranks * stride) % SN_COL).astype(jnp.int32)


def draw_shard_counts(key, part):
    first_key, second_key = jax.random.split(key)
    drawn_counts = jax.random.randint(first_key, (LAYERS * SECTORS,), HIT_DEV // 8, HIT_DEV + 1)
    position = jax.random.randint(second_key, (), 0, LAYERS * SECTORS)
    return drawn_counts.at[position].set(HIT_DEV).reshape(LAYERS, SECTORS).astype(jnp.int32)


def place_ends(drawn, stream_key, least, high):
    longest = drawn.shape.index(max(drawn.shape))
    spots = []
    for shift in (0, 1):
        where = [jax.random.randint(jax.random.fold_in(stream_key, axis), (), 0, length) for axis, length in enumerate(drawn.shape)]
        where[longest] = (where[longest] + shift) % drawn.shape[longest]
        spots.append(tuple(where))
    return drawn.at[spots[0]].set(least).at[spots[1]].set(high)


def levels(stream_key, extent, cuts, smallest, top_value):
    level, own = 1.0, jax.random.fold_in(stream_key, 6)
    for dim, shards_of in cuts:
        heights = jnp.exp(jax.random.uniform(jax.random.fold_in(own, dim), (shards_of,), jnp.float32, smallest / len(cuts), top_value / len(cuts)))
        level = level * jnp.repeat(heights, extent[dim] // shards_of).reshape([-1 if axis == dim else 1 for axis in range(len(extent))])
    return level


def centred(stream_key, extent, width, most, shards=(), kind=jnp.bfloat16):
    factor_of = levels(stream_key, extent, shards, -0.22, 0.18) if shards else 1.0
    result = jax.random.normal(stream_key, extent, jnp.float32) * width * factor_of
    return jnp.minimum(jnp.maximum(result, -most), most).astype(kind)


def setup_inputs(seed: int = 0) -> dict:
    arg_keys = jax.random.split(jax.random.key(seed), 10)
    return {
        "hits": centred(arg_keys[0], (LAYERS, SECTORS, HIT_DEV, WIDTH), 1.0, 6.0, ((0, 4), (1, 8))),
        "attach_index": draw_attach_index(jax.random.fold_in(arg_keys[9], 71), 0),
        "attach_weight": jnp.clip(jnp.exp(math.log(1.0) - 2.9996462 * jax.random.uniform(arg_keys[2], (LAYERS, SECTORS, 4, HIT_DEV), jnp.float32) ** levels(arg_keys[2], (LAYERS, SECTORS, 4, HIT_DEV), ((0, 4), (1, 8)), -0.2, 0.2)), 0.049804688, 1.0).astype(jnp.bfloat16),
        "shard_counts": draw_shard_counts(jax.random.fold_in(arg_keys[9], 71), 0),
        "edge_source": place_ends(jax.random.randint(arg_keys[4], (SECTORS, DEG, SN_COL), 0, SN_COL + 2 * RIM), jax.random.fold_in(arg_keys[4], 1), 0, (SN_COL + 2 * RIM) - 1).astype(jnp.int32),
        "cotangent": centred(arg_keys[5], (SECTORS, SN_COL, WIDTH), 2.0, 12.0, ((0, 8),)),
        "w_message": centred(arg_keys[6], (WIDTH, WIDTH), WIDTH ** -0.5, 0.5),
        "w_edge": centred(arg_keys[7], (WIDTH, WIDTH), WIDTH ** -0.5, 0.5),
        "w_output": centred(arg_keys[8], (WIDTH, WIDTH), WIDTH ** -0.5, 0.5),
    }


def silu_parts(preact):
    sigma = jax.nn.sigmoid(preact)
    return (preact * sigma, sigma * (1.0 + preact * (1.0 - sigma)))

def reference(hits, attach_index, attach_weight, shard_counts, edge_source, cotangent, w_message, w_edge, w_output):
    positions = jnp.arange(HIT_DEV, dtype=jnp.int32)

    def column_inputs(column):
        hit_block = lax.dynamic_index_in_dim(hits, column, 1, False).reshape(-1, WIDTH)
        index_block = jnp.transpose(lax.dynamic_index_in_dim(attach_index, column, 1, False), (0, 2, 1)).reshape(-1, 4)
        weight_block = jnp.transpose(lax.dynamic_index_in_dim(attach_weight, column, 1, False), (0, 2, 1)).reshape(-1, 4).astype(jnp.float32)
        count_block = lax.dynamic_index_in_dim(shard_counts, column, 1, False)
        realness = (positions[None, :] < count_block[:, None]).reshape(-1).astype(jnp.float32)
        message = jnp.tanh(jnp.dot(hit_block, w_message, preferred_element_type=jnp.float32)).astype(jnp.bfloat16)
        return (hit_block, index_block, weight_block * realness[:, None], message)

    def pool_column(column):
        hit_block, index_block, weight_block, message = column_inputs(column)
        terms = weight_block[:, :, None] * message.astype(jnp.float32)[:, None, :]
        pooled = jax.ops.segment_sum(terms.reshape(-1, WIDTH), index_block.reshape(-1), num_segments=SN_COL)
        masses = jax.ops.segment_sum(weight_block.reshape(-1), index_block.reshape(-1), num_segments=SN_COL)
        return (pooled, masses)
    sectors_iota = jnp.arange(SECTORS, dtype=jnp.int32)
    pooled, masses = lax.map(pool_column, sectors_iota)
    scale = (1.0 / jnp.sqrt(1.0 + masses)).astype(jnp.bfloat16)
    node = (pooled * scale.astype(jnp.float32)[:, :, None]).astype(jnp.bfloat16)
    preact = jnp.einsum('pnc,cd->pnd', node.astype(jnp.float32), w_edge.astype(jnp.float32))
    edge_act, edge_slope = silu_parts(preact)
    edge_msg = edge_act.astype(jnp.bfloat16)
    extended = jnp.concatenate([jnp.roll(edge_msg, 1, 0)[:, SN_COL - RIM:], edge_msg, jnp.roll(edge_msg, -1, 0)[:, :RIM]], axis=1)

    def gather_column(ext_col, src_col):
        return lax.optimization_barrier(jnp.sum(jnp.take(ext_col.astype(jnp.float32), src_col, axis=0), axis=0))
    gathered = jax.vmap(gather_column)(extended, edge_source).astype(jnp.bfloat16)
    d_gathered = jnp.einsum('pnc,dc->pnd', cotangent.astype(jnp.float32), w_output.astype(jnp.float32)).astype(jnp.bfloat16)
    node_norm = math.sqrt(SECTORS * SN_COL)
    grad_output = jnp.einsum('pnc,pnd->cd', gathered.astype(jnp.float32), cotangent.astype(jnp.float32)) / node_norm

    def spread_column(d_col, src_col):
        copies = jnp.broadcast_to(d_col.astype(jnp.float32)[None], (DEG, SN_COL, WIDTH)).reshape(-1, WIDTH)
        return jax.ops.segment_sum(copies, src_col.reshape(-1), num_segments=SN_COL + 2 * RIM)
    spread = jax.vmap(spread_column)(d_gathered, edge_source)
    d_edge = spread[:, RIM:RIM + SN_COL]
    d_edge = d_edge.at[:, SN_COL - RIM:].add(jnp.roll(spread, -1, 0)[:, :RIM])
    d_edge = d_edge.at[:, :RIM].add(jnp.roll(spread, 1, 0)[:, SN_COL + RIM:])
    d_pre = (d_edge * edge_slope).astype(jnp.bfloat16)
    grad_edge = jnp.einsum('pnc,pnd->cd', node.astype(jnp.float32), d_pre.astype(jnp.float32)) / node_norm
    back_node = jnp.einsum('pnd,cd->pnc', d_pre.astype(jnp.float32), w_edge.astype(jnp.float32))
    d_node = ((cotangent.astype(jnp.float32) + back_node) * scale.astype(jnp.float32)[:, :, None]).astype(jnp.bfloat16)

    def back_column(column):
        hit_block, index_block, weight_block, message = column_inputs(column)
        node_col = lax.dynamic_index_in_dim(d_node, column, 0, False).astype(jnp.float32)
        picked = jnp.take(node_col, index_block.reshape(-1), axis=0).reshape(-1, 4, WIDTH)
        d_message = lax.optimization_barrier(jnp.sum(weight_block[:, :, None] * picked, axis=1))
        message_f = message.astype(jnp.float32)
        d_act = (d_message * (1.0 - message_f * message_f)).astype(jnp.bfloat16)
        d_block = jnp.dot(d_act, w_message.T, preferred_element_type=jnp.float32).astype(jnp.bfloat16)
        term = jnp.dot(hit_block.T, d_act, preferred_element_type=jnp.float32)
        return (d_block.reshape(LAYERS, HIT_DEV, WIDTH), term)
    d_columns, terms = lax.map(back_column, sectors_iota)
    d_hits = jnp.transpose(d_columns, (1, 0, 2, 3))
    grad_message = lax.optimization_barrier(jnp.sum(terms, axis=0)) / math.sqrt(LAYERS * SECTORS * HIT_DEV)
    return (d_hits, grad_message, grad_edge, grad_output)
```

```python
import functools
import math

import jax
import jax.numpy as jnp
from jax import lax
from jax.experimental import pallas as pl
from jax.experimental.pallas import tpu as pltpu
from jax.sharding import PartitionSpec as P

BF = jnp.bfloat16
F32 = jnp.float32
LANES = 128
PACK = 16


def dot(a, b):
    return jnp.dot(a, b, preferred_element_type=F32)


def dot_nt(a, b):
    return lax.dot_general(a, b, (((1,), (1,)), ((), ())), preferred_element_type=F32)


def dot_tn(a, b):
    return lax.dot_general(a, b, (((0,), (0,)), ((), ())), preferred_element_type=F32)


def rows_of(values, j):
    return jnp.broadcast_to(values[j : j + 1], (PACK, values.shape[1])).astype(BF)


class Peers:
    def __init__(self, layers, sectors):
        self.n = {"layer": layers, "phi": sectors}
        self.me = {"layer": lax.axis_index("layer"), "phi": lax.axis_index("phi")}

    def at(self, axis, distance):
        n = self.n[axis]
        there = lax.rem(self.me[axis] + (distance + n) % n, n)
        if axis == "layer":
            return (there, self.me["phi"])
        return (self.me["layer"], there)


def send(src, dst, send_sem, recv_sem, device):
    copy = pltpu.make_async_remote_copy(
        src_ref=src,
        dst_ref=dst,
        send_sem=send_sem,
        recv_sem=recv_sem,
        device_id=device,
        device_id_type=pl.DeviceIdType.MESH,
    )
    copy.start()
    return copy


class AllReduce:
    def __init__(self, peers, refs):
        self.peers = peers
        self.mine, self.got, self.part, self.full, self.sems = refs
        self.copies = []

    def _send(self, src, dst, k, device):
        copy = send(src, dst, self.sems.at[0, k], self.sems.at[1, k], device)
        self.copies.append(copy)
        return copy

    def start(self, values):
        sectors = self.peers.n["phi"]
        rows = self.mine.shape[1]
        for p in range(sectors):
            self.mine[p] = values[p * rows : (p + 1) * rows]
        me = self.peers.me["phi"]
        self.now = [
            self._send(
                self.mine.at[lax.rem(me + d, sectors)],
                self.got.at[d - 1],
                d - 1,
                self.peers.at("phi", d),
            )
            for d in range(1, sectors)
        ]

    def exchange(self):
        sectors, layers = self.peers.n["phi"], self.peers.n["layer"]
        for copy in self.now:
            copy.wait_recv()
        total = self.mine[self.peers.me["phi"]]
        for d in range(sectors - 1):
            total = total + self.got[d]
        me = self.peers.me["layer"]
        self.part[me] = total
        self.now = [
            self._send(
                self.part.at[me],
                self.part.at[me],
                sectors - 1 + d - 1,
                self.peers.at("layer", d),
            )
            for d in range(1, layers)
        ]

    def gather(self):
        sectors, layers = self.peers.n["phi"], self.peers.n["layer"]
        for copy in self.now:
            copy.wait_recv()
        total = self.part[0]
        for k in range(1, layers):
            total = total + self.part[k]
        me = self.peers.me["phi"]
        self.full[me] = total
        self.now = [
            self._send(
                self.full.at[me],
                self.full.at[me],
                sectors + layers - 2 + d - 1,
                self.peers.at("phi", d),
            )
            for d in range(1, sectors)
        ]

    def finish(self):
        for copy in self.now:
            copy.wait_recv()
        for copy in self.copies:
            copy.wait_send()


def kernel(
    layers,
    sectors,
    chunk,
    hits,
    index,
    weight,
    count,
    source,
    cot,
    w_message,
    w_edge,
    w_output,
    d_hits,
    g_message,
    g_edge,
    g_output,
    tile,
    message,
    message_t,
    iota,
    rim_out,
    rim_in,
    rim_sems,
    pool_out,
    pool_in,
    pool_sems,
    back_out,
    back_in,
    back_sems,
    early_mine,
    early_got,
    early_part,
    early_full,
    early_sems,
    late_mine,
    late_got,
    late_part,
    late_full,
    late_sems,
):
    peers = Peers(layers, sectors)
    me_l = peers.me["layer"]
    hit_rows = hits.shape[0]
    width = hits.shape[1]
    nodes = cot.shape[0]
    rim = nodes // 2
    share = nodes // layers
    groups = share // PACK
    chunks = hit_rows // chunk

    barrier = pltpu.get_barrier_semaphore()
    for axis in ("layer", "phi"):
        for d in range(1, peers.n[axis]):
            pl.semaphore_signal(
                barrier,
                inc=1,
                device_id=peers.at(axis, d),
                device_id_type=pl.DeviceIdType.MESH,
            )

    iota[...] = (
        (
            lax.broadcasted_iota(jnp.int32, (groups, PACK, LANES), 0) * PACK
            + lax.broadcasted_iota(jnp.int32, (groups, PACK, LANES), 1)
        )
        .astype(F32)
        .astype(BF)
    )

    upper = me_l // (layers // 2)

    def spread_share(base):
        parts = []
        for c in range(nodes // LANES):
            rows = (source[:, c * LANES : (c + 1) * LANES] - base).astype(F32)
            total = None
            for j in range(source.shape[0]):
                hit = jnp.where(iota[...] == rows_of(rows, j)[None], BF(1), BF(0))
                total = hit if total is None else total + hit
            parts.append(total.reshape(share, LANES))
        return dot(jnp.concatenate(parts, axis=1), cot[...])

    rim_out[...] = spread_share(
        me_l * share + (1 - upper) * (nodes + rim) - upper * rim
    ).astype(BF)

    pl.semaphore_wait(barrier, layers - 1 + sectors - 1)

    target = lax.rem(peers.me["phi"] + sectors + 1 - 2 * upper, sectors)
    rim_copy = send(rim_out, rim_in, rim_sems.at[0], rim_sems.at[1], (me_l, target))
    own_spread = spread_share(me_l * share + rim)

    def message_step(k, carry):
        at = pl.ds(pl.multiple_of(k * chunk, chunk), chunk)
        msg = jnp.tanh(dot(hits[at, :], w_message[...])).astype(BF)
        message[at, :width] = msg
        message[at, width:] = jnp.ones((chunk, LANES), BF)
        message_t[:, at] = msg.T
        return carry

    lax.fori_loop(0, chunks, message_step, 0)

    real_count = count[0, 0]

    def pool_share(e):
        base = lax.rem(me_l + e, layers) * share

        def step(k, acc):
            start = pl.multiple_of(k * chunk, chunk)
            for c in range(chunk // LANES):
                at = pl.ds(pl.multiple_of(start + c * LANES, LANES), LANES)
                rows = (index[:, at] - base).astype(F32)
                position = start + c * LANES + lax.broadcasted_iota(jnp.int32, rows.shape, 1)
                wts = jnp.where(position < real_count, weight[:, at].astype(F32), 0.0)
                total = jnp.zeros((groups, PACK, LANES), BF)
                for j in range(index.shape[0]):
                    total = jnp.where(
                        iota[...] == rows_of(rows, j)[None],
                        jnp.broadcast_to(rows_of(wts, j)[None], total.shape),
                        total,
                    )
                tile[e, :, at] = total.reshape(share, LANES)
            at = pl.ds(start, chunk)
            return acc + dot(tile[e, :, at], message[at, :])

        return lax.fori_loop(0, chunks, step, jnp.zeros((share, width + LANES), F32))

    pool_copies = []
    for e in range(1, layers):
        pool_out[e - 1] = pool_share(e).astype(BF)
        pool_copies.append(
            send(
                pool_out.at[e - 1],
                pool_in.at[e - 1],
                pool_sems.at[0, e - 1],
                pool_sems.at[1, e - 1],
                peers.at("layer", e),
            )
        )
    total = pool_share(0)
    for e, copy in enumerate(pool_copies):
        copy.wait_recv()
        total = total + pool_in[e].astype(F32)

    scale = (1.0 / jnp.sqrt(1.0 + total[:, width:])).astype(BF).astype(F32)
    node = (total[:, :width] * scale).astype(BF)
    pre = dot(node, w_edge[...])
    sigma = jax.nn.sigmoid(pre)
    rim_copy.wait_recv()
    spread = (own_spread + rim_in[...].astype(F32)).astype(BF)
    d_edge = dot_nt(spread, w_output[...])
    d_pre = (d_edge * (sigma * (1.0 + pre * (1.0 - sigma)))).astype(BF)
    own_cot = cot[pl.ds(pl.multiple_of(me_l * share, share), share), :].astype(F32)
    d_node = ((own_cot + dot_nt(d_pre, w_edge[...])) * scale).astype(BF)
    back_out[...] = d_node.T
    back_copies = [
        send(
            back_out,
            back_in.at[d - 1],
            back_sems.at[0, d - 1],
            back_sems.at[1, d - 1],
            peers.at("layer", d),
        )
        for d in range(1, layers)
    ]
    early = AllReduce(peers, (early_mine, early_got, early_part, early_full, early_sems))
    edge_msg = (pre * sigma).astype(BF)
    early.start(jnp.concatenate([dot_tn(node, d_pre), dot_tn(edge_msg, spread)], axis=0))

    for copy in back_copies:
        copy.wait_recv()
    d_nodes = jnp.concatenate(
        [back_out[...]] + [back_in[layers - e - 1] for e in range(1, layers)], axis=1
    )

    def back_step(k, acc):
        at = pl.ds(pl.multiple_of(k * chunk, chunk), chunk)
        tiles = jnp.concatenate([tile[e, :, at] for e in range(layers)], axis=0)
        d_message = dot(d_nodes, tiles)
        msg = message_t[:, at].astype(F32)
        d_act = (d_message * (1.0 - msg * msg)).astype(BF)
        d_hits[at, :] = dot_nt(d_act.T, w_message[...]).astype(BF)
        return acc + dot(d_act, hits[at, :])

    cuts = [chunks * i // 4 for i in range(5)]
    stages = [early.exchange, early.gather, early.finish, lambda: None]
    acc = jnp.zeros((width, width), F32)
    for i, stage in enumerate(stages):
        acc = lax.fori_loop(cuts[i], cuts[i + 1], back_step, acc)
        stage()

    late = AllReduce(peers, (late_mine, late_got, late_part, late_full, late_sems))
    late.start(acc.T)
    rim_copy.wait_send()
    for copy in pool_copies + back_copies:
        copy.wait_send()
    node_norm = math.sqrt(sectors * nodes)
    half = early_full.shape[0] // 2
    rows = early_full.shape[1]
    for p in range(half):
        g_edge[p * rows : (p + 1) * rows] = early_full[p] / node_norm
        g_output[p * rows : (p + 1) * rows] = early_full[half + p] / node_norm
    late.exchange()
    late.gather()
    late.finish()
    hit_norm = math.sqrt(layers * sectors * hit_rows)
    rows = late_full.shape[1]
    for p in range(sectors):
        g_message[p * rows : (p + 1) * rows] = late_full[p] / hit_norm


def reduce_scratch(layers, sectors, rows):
    part = rows // sectors
    return [
        pltpu.VMEM((sectors, part, LANES), F32),
        pltpu.VMEM((sectors - 1, part, LANES), F32),
        pltpu.VMEM((layers, part, LANES), F32),
        pltpu.VMEM((sectors, part, LANES), F32),
        pltpu.SemaphoreType.DMA((2, 2 * (sectors - 1) + layers - 1)),
    ]


def shards(hits, index, weight, counts, source, cot, w_message, w_edge, w_output):
    layers, sectors = lax.axis_size("layer"), lax.axis_size("phi")
    hit_rows, width = hits.shape[2:]
    nodes = cot.shape[1]
    share = nodes // layers
    vmem = pl.BlockSpec(memory_space=pltpu.VMEM)
    out = pl.pallas_call(
        functools.partial(kernel, layers, sectors, min(1024, hit_rows)),
        out_shape=(
            jax.ShapeDtypeStruct((hit_rows, width), BF),
            jax.ShapeDtypeStruct((width, width), F32),
            jax.ShapeDtypeStruct((width, width), F32),
            jax.ShapeDtypeStruct((width, width), F32),
        ),
        in_specs=[vmem, vmem, vmem, pl.BlockSpec(memory_space=pltpu.SMEM)] + [vmem] * 5,
        out_specs=(vmem, vmem, vmem, vmem),
        scratch_shapes=[
            pltpu.VMEM((layers, share, hit_rows), BF),
            pltpu.VMEM((hit_rows, width + LANES), BF),
            pltpu.VMEM((width, hit_rows), BF),
            pltpu.VMEM((share // PACK, PACK, LANES), BF),
            pltpu.VMEM((share, width), BF),
            pltpu.VMEM((share, width), BF),
            pltpu.SemaphoreType.DMA((2,)),
            pltpu.VMEM((layers - 1, share, width + LANES), BF),
            pltpu.VMEM((layers - 1, share, width + LANES), BF),
            pltpu.SemaphoreType.DMA((2, layers - 1)),
            pltpu.VMEM((width, share), BF),
            pltpu.VMEM((layers - 1, width, share), BF),
            pltpu.SemaphoreType.DMA((2, layers - 1)),
        ]
        + reduce_scratch(layers, sectors, 2 * width)
        + reduce_scratch(layers, sectors, width),
        compiler_params=pltpu.CompilerParams(
            collective_id=0, has_side_effects=True, vmem_limit_bytes=56 * 1024 * 1024
        ),
    )(
        hits[0, 0],
        index[0, 0],
        weight[0, 0],
        counts,
        source[0],
        cot[0],
        w_message,
        w_edge,
        w_output,
    )
    return (out[0][None, None],) + tuple(out[1:])


def solution(mesh):
    placed = (
        P("layer", "phi", None, None),
        P("layer", "phi", None, None),
        P("layer", "phi", None, None),
        P("layer", "phi"),
        P("phi", None, None),
        P("phi", None, None),
        P(),
        P(),
        P(),
    )
    return jax.shard_map(
        shards,
        mesh=mesh,
        in_specs=placed,
        out_specs=(P("layer", "phi", None, None), P(), P(), P()),
        check_vma=False,
    )
```

```python
import functools
import math

import jax
import jax.numpy as jnp
from jax import lax
from jax.experimental import pallas as pl
from jax.experimental.pallas import tpu as pltpu
from jax.sharding import PartitionSpec as P

BF = jnp.bfloat16
F32 = jnp.float32
LANES = 128
PACK = 16


def dot(a, b):
    return jnp.dot(a, b, preferred_element_type=F32)


def dot_nt(a, b):
    return lax.dot_general(a, b, (((1,), (1,)), ((), ())), preferred_element_type=F32)


def dot_tn(a, b):
    return lax.dot_general(a, b, (((0,), (0,)), ((), ())), preferred_element_type=F32)


def rows_of(values, j, dtype):
    return jnp.broadcast_to(values[j : j + 1], (PACK, values.shape[1])).astype(dtype)


class Peers:
    def __init__(self, layers, sectors):
        self.n = {"layer": layers, "phi": sectors}
        self.me = {"layer": lax.axis_index("layer"), "phi": lax.axis_index("phi")}

    def at(self, axis, distance):
        n = self.n[axis]
        there = lax.rem(self.me[axis] + distance, n)
        if axis == "layer":
            return (there, self.me["phi"])
        return (self.me["layer"], there)


def remote(src, dst, send_sem, recv_sem, device):
    return pltpu.make_async_remote_copy(
        src_ref=src,
        dst_ref=dst,
        send_sem=send_sem,
        recv_sem=recv_sem,
        device_id=device,
        device_id_type=pl.DeviceIdType.MESH,
    )


def send(*what):
    copy = remote(*what)
    copy.start()
    return copy


class AllReduce:
    def __init__(self, peers, refs):
        self.peers = peers
        self.mine, self.got, self.part, self.full, self.sems = refs
        self.copies = []

    def _send(self, src, dst, k, device):
        copy = send(src, dst, self.sems.at[0, k], self.sems.at[1, k], device)
        self.copies.append(copy)
        return copy

    def start(self, values):
        sectors = self.peers.n["phi"]
        rows = self.mine.shape[1]
        for p in range(sectors):
            self.mine[p] = values[p * rows : (p + 1) * rows]
        me = self.peers.me["phi"]
        self.now = [
            self._send(
                self.mine.at[lax.rem(me + d, sectors)],
                self.got.at[d - 1],
                d - 1,
                self.peers.at("phi", d),
            )
            for d in range(1, sectors)
        ]

    def exchange(self):
        sectors, layers = self.peers.n["phi"], self.peers.n["layer"]
        for copy in self.now:
            copy.wait_recv()
        total = self.mine[self.peers.me["phi"]]
        for d in range(sectors - 1):
            total = total + self.got[d]
        me = self.peers.me["layer"]
        self.part[me] = total
        self.now = [
            self._send(
                self.part.at[me],
                self.part.at[me],
                sectors - 1 + d - 1,
                self.peers.at("layer", d),
            )
            for d in range(1, layers)
        ]

    def gather(self):
        sectors, layers = self.peers.n["phi"], self.peers.n["layer"]
        for copy in self.now:
            copy.wait_recv()
        total = self.part[0]
        for k in range(1, layers):
            total = total + self.part[k]
        me = self.peers.me["phi"]
        self.full[me] = total
        self.now = [
            self._send(
                self.full.at[me],
                self.full.at[me],
                sectors + layers - 2 + d - 1,
                self.peers.at("phi", d),
            )
            for d in range(1, sectors)
        ]

    def finish(self):
        for copy in self.now:
            copy.wait_recv()
        for copy in self.copies:
            copy.wait_send()


def kernel(
    layers,
    sectors,
    chunk,
    hits,
    index,
    weight,
    count,
    source,
    cot,
    w_message,
    w_edge,
    w_output,
    d_hits,
    g_message,
    g_edge,
    g_output,
    tile_a,
    tile_b,
    pooled,
    node_rows,
    weight_rows,
    message,
    message_t,
    iota,
    rim_out,
    rim_in,
    rim_sems,
    pool_out,
    pool_in,
    pool_sems,
    back_out,
    back_in,
    back_sems,
    early_mine,
    early_got,
    early_part,
    early_full,
    early_sems,
    late_mine,
    late_got,
    late_part,
    late_full,
    late_sems,
):
    peers = Peers(layers, sectors)
    me_l = peers.me["layer"]
    hit_rows = hits.shape[0]
    width = hits.shape[1]
    nodes = cot.shape[0]
    rim = nodes // 2
    share = nodes // layers
    groups = share // PACK
    chunks = hit_rows // chunk

    barrier = pltpu.get_barrier_semaphore()
    for axis in ("layer", "phi"):
        for d in range(1, peers.n[axis]):
            pl.semaphore_signal(
                barrier,
                inc=1,
                device_id=peers.at(axis, d),
                device_id_type=pl.DeviceIdType.MESH,
            )

    iota[...] = (
        (
            lax.broadcasted_iota(jnp.int32, (groups, PACK, LANES), 0) * PACK
            + lax.broadcasted_iota(jnp.int32, (groups, PACK, LANES), 1)
        )
        .astype(jnp.int16)
    )

    upper = me_l // (layers // 2)

    def spread_share(base):
        parts = []
        for c in range(nodes // LANES):
            rows = source[:, c * LANES : (c + 1) * LANES] - base
            total = None
            for j in range(source.shape[0]):
                hit = jnp.where(iota[...] == rows_of(rows, j, jnp.int16)[None], BF(1), BF(0))
                total = hit if total is None else total + hit
            parts.append(total.reshape(share, LANES))
        return dot(jnp.concatenate(parts, axis=1), cot[...])

    rim_out[...] = spread_share(
        me_l * share + (1 - upper) * (nodes + rim) - upper * rim
    ).astype(BF)

    target = lax.rem(peers.me["phi"] + sectors + 1 - 2 * upper, sectors)
    rim_copy = remote(rim_out, rim_in, rim_sems.at[0], rim_sems.at[1], (me_l, target))
    own_spread = spread_share(me_l * share + rim)

    real_count = count[0, 0]

    def message_step(k, carry):
        at = pl.ds(pl.multiple_of(k * chunk, chunk), chunk)
        msg = jnp.tanh(dot(hits[at, :], w_message[...])).astype(BF)
        message[at, :width] = msg
        message[at, width:] = jnp.ones((chunk, LANES), BF)
        message_t[:, at] = msg.T
        position = k * chunk + lax.broadcasted_iota(jnp.int32, (4, chunk), 1)
        weights = jnp.where(position < real_count, weight[:, at].astype(F32), 0.0)
        nodes_of = index[:, at]
        for j in range(4):
            node_rows[j, :, at] = rows_of(nodes_of, j, jnp.int16)
            weight_rows[j, :, at] = rows_of(weights, j, BF)
        return carry

    lax.fori_loop(0, chunks, message_step, 0)

    pairs = chunks // 2
    slots = index.shape[0]

    def build(tile, e, i, k):
        base = (lax.rem(me_l + e, layers) * share).astype(jnp.int16)
        for c in range(chunk // LANES):
            at = pl.ds(pl.multiple_of(k * chunk + c * LANES, LANES), LANES)
            total = jnp.zeros((groups, PACK, LANES), BF)
            for j in range(slots):
                total = jnp.where(
                    iota[...] == (node_rows[j, :, at] - base)[None],
                    jnp.broadcast_to(weight_rows[j, :, at][None], total.shape),
                    total,
                )
            to = pl.ds(pl.multiple_of(i * chunk + c * LANES, LANES), LANES)
            tile[e, :, to] = total.reshape(share, LANES)

    def use(tile, e, i, k):
        of = pl.ds(pl.multiple_of(i * chunk, chunk), chunk)
        at = pl.ds(pl.multiple_of(k * chunk, chunk), chunk)
        pooled[...] += dot(tile[e, :, of], message[at, :])

    def pool_copy(e):
        return remote(
            pool_out.at[e - 1],
            pool_in.at[e - 1],
            pool_sems.at[0, e - 1],
            pool_sems.at[1, e - 1],
            peers.at("layer", e),
        )

    build(tile_a, 1, 0, 0)

    def pool_share(step, carry):
        e = lax.rem(step, layers)
        pooled[...] = jnp.zeros_like(pooled)

        def pair(i, carry):
            after = i + 1
            wrap = after // pairs
            after = after - wrap * pairs
            build(tile_b, e, i, 2 * i + 1)
            use(tile_a, e, i, 2 * i)
            build(tile_a, lax.rem(step + wrap, layers), after, 2 * after)
            use(tile_b, e, i, 2 * i + 1)
            return carry

        lax.fori_loop(0, pairs, pair, 0)

        @pl.when(step == 1)
        def _():
            pl.semaphore_wait(barrier, layers - 1 + sectors - 1)
            rim_copy.start()

        @pl.when(step < layers)
        def _():
            pool_out[step - 1] = pooled[...].astype(BF)
            pool_copy(step).start()

        return carry

    lax.fori_loop(1, layers + 1, pool_share, 0)
    pool_copies = [pool_copy(e) for e in range(1, layers)]
    total = pooled[...]
    for e, copy in enumerate(pool_copies):
        copy.wait_recv()
        total = total + pool_in[e].astype(F32)

    scale = (1.0 / jnp.sqrt(1.0 + total[:, width:])).astype(BF).astype(F32)
    node = (total[:, :width] * scale).astype(BF)
    pre = dot(node, w_edge[...])
    sigma = jax.nn.sigmoid(pre)
    rim_copy.wait_recv()
    spread = (own_spread + rim_in[...].astype(F32)).astype(BF)
    d_edge = dot_nt(spread, w_output[...])
    d_pre = (d_edge * (sigma * (1.0 + pre * (1.0 - sigma)))).astype(BF)
    own_cot = cot[pl.ds(pl.multiple_of(me_l * share, share), share), :].astype(F32)
    d_node = ((own_cot + dot_nt(d_pre, w_edge[...])) * scale).astype(BF)
    back_out[...] = d_node.T
    back_copies = [
        send(
            back_out,
            back_in.at[d - 1],
            back_sems.at[0, d - 1],
            back_sems.at[1, d - 1],
            peers.at("layer", d),
        )
        for d in range(1, layers)
    ]
    early = AllReduce(peers, (early_mine, early_got, early_part, early_full, early_sems))
    edge_msg = (pre * sigma).astype(BF)
    early.start(jnp.concatenate([dot_tn(node, d_pre), dot_tn(edge_msg, spread)], axis=0))

    for copy in back_copies:
        copy.wait_recv()
    d_nodes = jnp.concatenate(
        [back_out[...]] + [back_in[layers - e - 1] for e in range(1, layers)], axis=1
    )

    def back_step(tile, i, k, acc):
        of = pl.ds(pl.multiple_of(i * chunk, chunk), chunk)
        at = pl.ds(pl.multiple_of(k * chunk, chunk), chunk)
        tiles = jnp.concatenate([tile[e, :, of] for e in range(layers)], axis=0)
        d_message = dot(d_nodes, tiles)
        msg = message_t[:, at].astype(F32)
        d_act = (d_message * (1.0 - msg * msg)).astype(BF)
        message_t[:, at] = d_act
        return acc + dot(d_act, hits[at, :])

    def back_pair(i, acc):
        acc = back_step(tile_a, i, 2 * i, acc)
        return back_step(tile_b, i, 2 * i + 1, acc)

    acc = lax.fori_loop(0, pairs, back_pair, jnp.zeros((width, width), F32))
    late = AllReduce(peers, (late_mine, late_got, late_part, late_full, late_sems))
    late.start(acc.T)
    early.exchange()

    def hit_step(k, carry):
        at = pl.ds(pl.multiple_of(k * chunk, chunk), chunk)
        d_hits[at, :] = dot_nt(message_t[:, at].T, w_message[...]).astype(BF)
        return carry

    cuts = [chunks * i // 3 for i in range(4)]
    lax.fori_loop(cuts[0], cuts[1], hit_step, 0)
    late.exchange()
    early.gather()
    lax.fori_loop(cuts[1], cuts[2], hit_step, 0)
    late.gather()
    early.finish()
    lax.fori_loop(cuts[2], cuts[3], hit_step, 0)
    rim_copy.wait_send()
    for copy in pool_copies + back_copies:
        copy.wait_send()
    node_norm = math.sqrt(sectors * nodes)
    half = early_full.shape[0] // 2
    rows = early_full.shape[1]
    for p in range(half):
        g_edge[p * rows : (p + 1) * rows] = early_full[p] / node_norm
        g_output[p * rows : (p + 1) * rows] = early_full[half + p] / node_norm
    late.finish()
    hit_norm = math.sqrt(layers * sectors * hit_rows)
    rows = late_full.shape[1]
    for p in range(sectors):
        g_message[p * rows : (p + 1) * rows] = late_full[p] / hit_norm


def reduce_scratch(layers, sectors, rows):
    part = rows // sectors
    return [
        pltpu.VMEM((sectors, part, LANES), F32),
        pltpu.VMEM((sectors - 1, part, LANES), F32),
        pltpu.VMEM((layers, part, LANES), F32),
        pltpu.VMEM((sectors, part, LANES), F32),
        pltpu.SemaphoreType.DMA((2, 2 * (sectors - 1) + layers - 1)),
    ]


def shards(hits, index, weight, counts, source, cot, w_message, w_edge, w_output):
    layers, sectors = lax.axis_size("layer"), lax.axis_size("phi")
    hit_rows, width = hits.shape[2:]
    nodes = cot.shape[1]
    share = nodes // layers
    vmem = pl.BlockSpec(memory_space=pltpu.VMEM)
    out = pl.pallas_call(
        functools.partial(kernel, layers, sectors, min(2048, hit_rows // 2)),
        out_shape=(
            jax.ShapeDtypeStruct((hit_rows, width), BF),
            jax.ShapeDtypeStruct((width, width), F32),
            jax.ShapeDtypeStruct((width, width), F32),
            jax.ShapeDtypeStruct((width, width), F32),
        ),
        in_specs=[vmem, vmem, vmem, pl.BlockSpec(memory_space=pltpu.SMEM)] + [vmem] * 5,
        out_specs=(vmem, vmem, vmem, vmem),
        scratch_shapes=[
            pltpu.VMEM((layers, share, hit_rows // 2), BF),
            pltpu.VMEM((layers, share, hit_rows // 2), BF),
            pltpu.VMEM((share, width + LANES), F32),
            pltpu.VMEM((4, PACK, hit_rows), jnp.int16),
            pltpu.VMEM((4, PACK, hit_rows), BF),
            pltpu.VMEM((hit_rows, width + LANES), BF),
            pltpu.VMEM((width, hit_rows), BF),
            pltpu.VMEM((share // PACK, PACK, LANES), jnp.int16),
            pltpu.VMEM((share, width), BF),
            pltpu.VMEM((share, width), BF),
            pltpu.SemaphoreType.DMA((2,)),
            pltpu.VMEM((layers - 1, share, width + LANES), BF),
            pltpu.VMEM((layers - 1, share, width + LANES), BF),
            pltpu.SemaphoreType.DMA((2, layers - 1)),
            pltpu.VMEM((width, share), BF),
            pltpu.VMEM((layers - 1, width, share), BF),
            pltpu.SemaphoreType.DMA((2, layers - 1)),
        ]
        + reduce_scratch(layers, sectors, 2 * width)
        + reduce_scratch(layers, sectors, width),
        compiler_params=pltpu.CompilerParams(
            collective_id=0, has_side_effects=True, vmem_limit_bytes=56 * 1024 * 1024
        ),
    )(
        hits[0, 0],
        index[0, 0],
        weight[0, 0],
        counts,
        source[0],
        cot[0],
        w_message,
        w_edge,
        w_output,
    )
    return (out[0][None, None],) + tuple(out[1:])


def solution(mesh):
    placed = (
        P("layer", "phi", None, None),
        P("layer", "phi", None, None),
        P("layer", "phi", None, None),
        P("layer", "phi"),
        P("phi", None, None),
        P("phi", None, None),
        P(),
        P(),
        P(),
    )
    return jax.shard_map(
        shards,
        mesh=mesh,
        in_specs=placed,
        out_specs=(P("layer", "phi", None, None), P(), P(), P()),
        check_vma=False,
    )
```
